512 devices in a mesh: replica: 64 (over x, y, z_lo), fsdp: 8 (over z_hi, core).
Axes of the slice: x: 4, y: 4, z: 16 (z_hi: 4, z_lo: 4; z = z_hi * 4 + z_lo), core: 2. Of those that a mesh axis runs over, the one named last changes fastest.
Arguments:
- tokens: bfloat16 [131072, 4096], P(('replica', 'fsdp')), may hold values from -6 to 6
- w_key: float32 [4096, 512], P('fsdp'), may hold values from -0.09375 to 0.09375
- targets: bfloat16 [131072, 512], P(('replica', 'fsdp')), may hold values from -6 to 6
- frag_outer: float32 [4096, 1024], P(('fsdp', 'replica')), may hold values from -6 to 6
- frag_local: bfloat16 [262144, 1024], P(('replica', 'fsdp')), may hold values from -6 to 6
- frag_moment: float32 [4096, 1024], P(('fsdp', 'replica')), may hold values from -6 to 6
Outputs:
- new_key: float32 [262144, 512], P(('replica', 'fsdp'))
- new_outer: float32 [4096, 1024], P(('fsdp', 'replica'))
- new_moment: float32 [4096, 1024], P(('fsdp', 'replica'))
The draws below stay inside these ranges and needn't reach their ends.
All inputs are finite; a program needn't handle non-finite values.
Results may differ from the reference program's by a relative error of at most 0.017.
Values may be sent and summed in bfloat16 or wider, within the bound.
No kernel may reach another device: no remote copies, remote signals or barrier semaphores. Data moves between devices by JAX's collectives and lax.ppermute only.
A program may use at most 64 MiB of HBM per device.

```python
import jax
import jax.numpy as jnp
from jax import lax

D = 4096
KW = 512
FB = 1024
TOK_DEV = 256
TOKENS = 131072
N_REPLICA = 64
N_FSDP = 8


def block_levels(key, shape, pieces, low, top_value):
    def one(position, parts):
        heights = jax.random.uniform(jax.random.fold_in(jax.random.fold_in(key, 6), position), (parts,), jnp.float32, low / len(pieces), top_value / len(pieces))
        return jnp.repeat(jnp.exp(heights), shape[position] // parts).reshape((-1,) + (1,) * (len(shape) - position - 1))

    factor_of = one(*pieces[0])
    for cut in pieces[1:]:
        factor_of = factor_of * one(*cut)
    return factor_of


def gaussian(stream_key, extent, deviation, reach, shards=(), kind=jnp.bfloat16):
    result = deviation * jax.random.normal(stream_key, extent, jnp.float32)
    if shards:
        result = result * block_levels(stream_key, extent, shards, -0.22, 0.18)
    return jnp.clip(result, -reach, reach).astype(kind)


def setup_inputs(seed: int = 0) -> dict:
    key_list = jax.random.split(jax.random.key(seed), 7)
    return {
        "tokens": gaussian(key_list[0], (TOKENS, D), 1.0, 6.0, ((0, 512),)),
        "w_key": gaussian(key_list[1], (D, KW), D ** -0.5, 0.09375, ((0, 8),), jnp.float32),
        "targets": gaussian(key_list[2], (TOKENS, KW), 1.0, 6.0, ((0, 512),)),
        "frag_outer": gaussian(key_list[3], (D, FB), 1.0, 6.0, ((0, 512),), jnp.float32),
        "frag_local": gaussian(key_list[4], (N_REPLICA * D, FB), 1.0, 6.0, ((0, 512),)),
        "frag_moment": gaussian(key_list[5], (D, FB), 0.5, 6.0, ((0, 512),), jnp.float32),
    }


INNER_RATE = 4.0
OUTER_RATE = 0.7
MOMENTUM = 0.9


def inner_step(args, key_b, w_key):
    rows, goal = args
    flat = rows.reshape(-1, D)
    keys = jnp.dot(flat, key_b, preferred_element_type=jnp.float32)
    errors = (keys - goal.reshape(-1, KW).astype(jnp.float32)).astype(jnp.bfloat16)
    partials = jnp.einsum("ktd,ktf->kdf", rows.astype(jnp.float32), errors.reshape(N_FSDP, TOK_DEV, KW).astype(jnp.float32))
    grad = lax.optimization_barrier(partials.astype(jnp.bfloat16)).astype(jnp.float32).sum(0)
    return w_key - (INNER_RATE / D) * grad


def reference(tokens, w_key, targets, frag_outer, frag_local, frag_moment):
    key_b = w_key.astype(jnp.bfloat16)
    grouped = tokens.reshape(N_REPLICA, N_FSDP, TOK_DEV, D)
    goals = targets.reshape(N_REPLICA, N_FSDP, TOK_DEV, KW)
    new_key = lax.map(lambda args: inner_step(args, key_b, w_key), (grouped, goals))
    total = jnp.sum(frag_local.reshape(N_REPLICA, D, FB), axis=0, dtype=jnp.float32)
    mean = frag_outer - total / N_REPLICA
    new_moment = MOMENTUM * frag_moment + mean
    new_outer = frag_outer - OUTER_RATE * (mean + MOMENTUM * new_moment)
    return (new_key.reshape(N_REPLICA * D, KW), new_outer, new_moment)
```

```python
import jax
import jax.numpy as jnp
from jax import lax
from jax.experimental import pallas as pl
from jax.experimental.pallas import tpu as pltpu
from jax.sharding import Mesh, PartitionSpec as P

INNER_RATE = 4.0
OUTER_RATE = 0.7
MOMENTUM = 0.9

X, Y, ZL, ZH = 4, 4, 4, 4
PARAMS = pltpu.CompilerParams(vmem_limit_bytes=40 * 1024 * 1024)
SWAP = [(0, 1), (1, 0)]


def shift(a, step):
    return lax.ppermute(a, "zh", [(i, (i + step) % ZH) for i in range(ZH)])


def transpose_kernel(place, own, mate, out):
    zh, core = place[0], place[1]
    width = out.shape[1]
    tokens = own.shape[0]
    for j in range(ZH):
        block = lax.rem(zh + j, ZH) * 2 + core
        columns = pl.ds(pl.multiple_of(block * width, width), width)
        out[j, :, :tokens] = own[:, columns].T
        out[j, :, tokens:] = mate[:, columns].T


def error_kernel(own, mate, w, goal_own, goal_mate, out):
    shards, depth = w.shape[1], w.shape[0] * w.shape[2]
    tokens = own.shape[0]
    width = w.shape[3]
    for half, (x, goal) in enumerate(((own, goal_own), (mate, goal_mate))):
        keys = jnp.zeros((tokens, width), jnp.float32)
        for f in range(shards):
            keys += jnp.dot(
                x[:, f * depth : (f + 1) * depth],
                w[:, f].reshape(depth, width),
                preferred_element_type=jnp.float32,
            )
        errors = keys - goal[...].astype(jnp.float32)
        out[half * tokens : (half + 1) * tokens, :] = errors.astype(jnp.bfloat16)


def gradient_kernel(place, xt, err_own, err_mate, first, second, third, own, *, order):
    core = place[1]
    tokens = err_own.shape[0] // 2
    mine = err_own[...]
    other = jnp.concatenate([err_mate[tokens:, :], err_mate[:tokens, :]], axis=0)
    low = jnp.where(core == 0, mine, other)
    high = jnp.where(core == 0, other, mine)
    errors = jnp.concatenate([low, high], axis=1)
    for j, out in zip(order, (first, second, third, own), strict=True):
        part = jnp.dot(xt[j], errors, preferred_element_type=jnp.float32)
        out[...] = part.astype(out.dtype)


def finish_kernel(w, own_a, own_b, plain_a, plain_b, sum_a, sum_b, out, *, rate):
    lanes = own_a.shape[1] // 2
    for h, (own, plain, total) in enumerate(((own_a, plain_a, sum_a), (own_b, plain_b, sum_b))):
        grad = own[...] + plain[...].astype(jnp.float32) + total[...].astype(jnp.float32)
        for core in range(2):
            at = (core * 2 + h) * lanes
            out[:, at : at + lanes] = w[:, at : at + lanes] - rate * grad[:, core * lanes : (core + 1) * lanes]


def on_device(tokens, w_key, targets, frag_outer, frag_local, frag_moment):
    rows, width = tokens.shape
    own_rows, columns = w_key.shape
    half, lanes = columns // 2, columns // 4
    spots = X * Y
    core = lax.axis_index("c")
    zh = lax.axis_index("zh")
    spot = lax.axis_index("x") * Y + lax.axis_index("y")
    place = jnp.stack([zh, core]).astype(jnp.int32)
    smem = pl.BlockSpec(memory_space=pltpu.SMEM)
    vmem = pl.BlockSpec(memory_space=pltpu.VMEM)

    piece = own_rows // spots
    mine = lax.dynamic_slice_in_dim(w_key, spot * piece, piece, 0).astype(jnp.bfloat16)
    column = lax.all_gather(mine, ("zh", "c"), axis=0, tiled=True)
    column = lax.dynamic_slice_in_dim(column, core * half, half, 1)
    column = column.reshape(ZH * 2, piece, 2, lanes)

    def spread(part):
        copies = jnp.broadcast_to(part[None], (spots,) + part.shape)
        return lax.all_to_all(copies, ("x", "y"), 0, 0, tiled=True)

    key_a = spread(column[:, :, 0])
    key_b = spread(column[:, :, 1])

    mate = lax.ppermute(tokens, "c", SWAP)
    for_mate = lax.dynamic_slice_in_dim(targets, (1 - core) * half, half, 1)
    goal_own = lax.dynamic_slice_in_dim(targets, core * half, half, 1)
    goal_mate = lax.ppermute(for_mate, "c", SWAP)
    xt = pl.pallas_call(
        transpose_kernel,
        out_shape=jax.ShapeDtypeStruct((ZH, own_rows, 2 * rows), jnp.bfloat16),
        in_specs=[smem, vmem, vmem],
        out_specs=vmem,
        compiler_params=PARAMS,
    )(place, tokens, mate)

    def errors(key, at):
        return pl.pallas_call(
            error_kernel,
            out_shape=jax.ShapeDtypeStruct((2 * rows, lanes), jnp.bfloat16),
            in_specs=[vmem] * 5,
            out_specs=vmem,
            compiler_params=PARAMS,
        )(tokens, mate, key, goal_own[:, at : at + lanes], goal_mate[:, at : at + lanes])

    def gradient(err, order):
        err_mate = lax.ppermute(err, "c", SWAP)
        short = jax.ShapeDtypeStruct((own_rows, half), jnp.bfloat16)
        full = jax.ShapeDtypeStruct((own_rows, half), jnp.float32)

        def kernel(*refs):
            gradient_kernel(*refs, order=order)

        return pl.pallas_call(
            kernel,
            out_shape=(short, short, full, full),
            in_specs=[smem] + [vmem] * 3,
            out_specs=(vmem,) * 4,
            compiler_params=PARAMS,
        )(place, xt, err, err_mate)

    far_a, near_a, via_a, own_a = gradient(errors(key_a, 0), (2, 3, 1, 0))
    far_a = shift(far_a, 1)
    plain_a = shift(near_a, -1)
    far_b, near_b, via_b, own_b = gradient(errors(key_b, lanes), (2, 1, 3, 0))
    far_b = shift(far_b, -1)
    plain_b = shift(near_b, 1)
    sum_a = shift((via_a + far_a.astype(jnp.float32)).astype(jnp.bfloat16), 1)
    sum_b = shift((via_b + far_b.astype(jnp.float32)).astype(jnp.bfloat16), -1)

    rate = INNER_RATE / width

    def finish(*refs):
        finish_kernel(*refs, rate=rate)

    new_key = pl.pallas_call(
        finish,
        out_shape=jax.ShapeDtypeStruct(w_key.shape, jnp.float32),
        in_specs=[vmem] * 7,
        out_specs=vmem,
        compiler_params=PARAMS,
    )(w_key, own_a, own_b, plain_a, plain_b, sum_a, sum_b)

    owned = frag_outer.shape[0]
    pieces = lax.all_to_all(frag_local, ("x", "y"), 0, 0, tiled=True)
    part = pieces.astype(jnp.float32).reshape(spots, ZL * owned, -1).sum(0)
    part = lax.all_to_all(part, "zl", 0, 0, tiled=True)
    total = part.reshape(ZL, owned, -1).sum(0)
    mean = frag_outer - total / (spots * ZL)
    new_moment = MOMENTUM * frag_moment + mean
    new_outer = frag_outer - OUTER_RATE * (mean + MOMENTUM * new_moment)
    return (new_key, new_outer, new_moment)


def solution(mesh):
    grid = Mesh(mesh.devices.reshape(X, Y, ZL, ZH, 2), ("x", "y", "zl", "zh", "c"))
    replica, fsdp = ("x", "y", "zl"), ("zh", "c")
    in_specs = (
        P(replica + fsdp, None),
        P(fsdp, None),
        P(replica + fsdp, None),
        P(fsdp + replica, None),
        P(replica + fsdp, None),
        P(fsdp + replica, None),
    )
    out_specs = (
        P(replica + fsdp, None),
        P(fsdp + replica, None),
        P(fsdp + replica, None),
    )
    return jax.shard_map(
        on_device, mesh=grid, in_specs=in_specs, out_specs=out_specs, check_vma=False
    )
```

```python
import functools

import jax
import jax.numpy as jnp
from jax import lax
from jax.experimental import pallas as pl
from jax.experimental.pallas import tpu as pltpu
from jax.sharding import Mesh, PartitionSpec as P

INNER_RATE = 4.0
OUTER_RATE = 0.7
MOMENTUM = 0.9

X, Y, ZL, ZH = 4, 4, 4, 4
PARAMS = pltpu.CompilerParams(vmem_limit_bytes=16 * 1024 * 1024)
SWAP = [(0, 1), (1, 0)]


def cost(flops, touched):
    return pl.CostEstimate(flops=flops, bytes_accessed=touched, transcendentals=0)


def shift(a, step):
    return lax.ppermute(a, "zh", [(i, (i + step) % ZH) for i in range(ZH)])


def transpose_kernel(place, own, mate, order, out, both):
    del order
    zh, core = place[0], place[1]
    width = out.shape[1]
    tokens = own.shape[0]
    both[:tokens] = own[...]
    both[tokens:] = mate[...]
    for j in range(ZH):
        block = lax.rem(zh + j, ZH) * 2 + core
        columns = pl.ds(pl.multiple_of(block * width, width), width)
        out[j, :, :tokens] = own[:, columns].T
        out[j, :, tokens:] = mate[:, columns].T


def spread_kernel(place, column, out):
    width = out.shape[3]
    at = place[1] * width
    part = column[:, pl.ds(pl.multiple_of(at, width), width)].reshape(out.shape[1:])
    for i in range(out.shape[0]):
        out[i] = part


def error_kernel(place, both, w, goal_own, goal_mate, out):
    shards, depth = w.shape[1], w.shape[0] * w.shape[2]
    tokens = goal_own.shape[0]
    width = w.shape[3]
    columns = pl.ds(pl.multiple_of(place[1] * width, width), width)
    for i, goal in enumerate((goal_own, goal_mate)):
        at = slice(i * tokens, (i + 1) * tokens)
        keys = jnp.zeros((tokens, width), jnp.float32)
        for f in range(shards):
            keys += jnp.dot(
                both[at, f * depth : (f + 1) * depth],
                w[:, f].reshape(depth, width),
                preferred_element_type=jnp.float32,
            )
        errors = keys - goal[:, columns].astype(jnp.float32)
        out[at, :] = errors.astype(jnp.bfloat16)


def errors_of(place, err_own, err_mate):
    tokens = err_own.shape[0] // 2
    mine = err_own[...]
    other = jnp.concatenate([err_mate[tokens:, :], err_mate[:tokens, :]], axis=0)
    low = jnp.where(place[1] == 0, mine, other)
    high = jnp.where(place[1] == 0, other, mine)
    return jnp.concatenate([low, high], axis=1)


def far_kernel(place, xt, err_own, err_mate, order, up, down):
    del order
    rows = up.shape[0]
    part = jnp.dot(xt[2], errors_of(place, err_own, err_mate), preferred_element_type=jnp.float32)
    up[...] = part[:rows].astype(up.dtype)
    down[...] = part[rows:].astype(down.dtype)


def near_kernel(place, xt, err_own, err_mate, w, part, order, up, down, base, same, *, rate):
    del order
    same[...] = part[...]
    errors = errors_of(place, err_own, err_mate)
    up[...] = jnp.dot(xt[1], errors, preferred_element_type=jnp.float32)
    down[...] = jnp.dot(xt[3], errors, preferred_element_type=jnp.float32)
    base[...] = w[...] - rate * jnp.dot(xt[0], errors, preferred_element_type=jnp.float32)


def pass_kernel(part, far, out, *, half):
    rows = far.shape[0]
    at, rest = half * rows, (1 - half) * rows
    out[:rows] = (part[at : at + rows] + far[...].astype(jnp.float32)).astype(out.dtype)
    out[rows:] = part[rest : rest + rows].astype(out.dtype)


def finish_kernel(base, up, down, out, *, rate):
    rows = up.shape[0] // 2
    for h, (total, plain) in enumerate(((up, down), (down, up))):
        at = slice(h * rows, (h + 1) * rows)
        grad = plain[rows:].astype(jnp.float32) + total[:rows].astype(jnp.float32)
        out[at, :] = base[at, :] - rate * grad


def sort_kernel(place, given, order, keep, one, two, three, held):
    del order
    spread, rows, wide = held.shape
    owned = given.shape[0] // (spread * X * Y)
    for at in range(0, rows, 2 * owned):
        block = given[at * spread : (at + 2 * owned) * spread].astype(jnp.float32)
        block = block.reshape(2, spread, owned, wide)
        for i in range(spread):
            held[i, at : at + 2 * owned] = block[:, i].reshape(2 * owned, wide).astype(held.dtype)
    for j, out in enumerate((keep, one, two, three)):
        out[...] = held[place[2] ^ j]


def reduce_kernel(keep, one, two, three, out):
    out[...] = (keep[...].astype(jnp.float32) + one[...].astype(jnp.float32)) + (
        two[...].astype(jnp.float32) + three[...].astype(jnp.float32)
    )


def on_device(tokens, w_key, targets, frag_outer, frag_local, frag_moment):
    rows, width = tokens.shape
    own_rows, columns = w_key.shape
    half = columns // 2
    spots = X * Y
    core = lax.axis_index("c")
    zh = lax.axis_index("zh")
    spot = lax.axis_index("x") * Y + lax.axis_index("y")
    place = jnp.stack([zh, core, lax.axis_index("zl")]).astype(jnp.int32)
    smem = pl.BlockSpec(memory_space=pltpu.SMEM)
    vmem = pl.BlockSpec(memory_space=pltpu.VMEM)
    anywhere = pl.BlockSpec(memory_space=pl.ANY)

    piece = own_rows // spots
    mine = lax.dynamic_slice_in_dim(w_key, spot * piece, piece, 0).astype(jnp.bfloat16)
    column = lax.all_gather(mine, ("zh", "c"), axis=0, tiled=True)
    copies = pl.pallas_call(
        spread_kernel,
        out_shape=jax.ShapeDtypeStruct((spots, ZH * 2, piece, half), jnp.bfloat16),
        in_specs=[smem, vmem],
        out_specs=vmem,
        compiler_params=PARAMS,
    )(place, column)
    key = lax.all_to_all(copies, ("x", "y"), 0, 0, tiled=True)

    mate = lax.ppermute(tokens, "c", SWAP)
    goal_mate = lax.ppermute(targets, "c", SWAP)
    xt, both = pl.pallas_call(
        transpose_kernel,
        out_shape=(
            jax.ShapeDtypeStruct((ZH, own_rows, 2 * rows), jnp.bfloat16),
            jax.ShapeDtypeStruct((2 * rows, width), jnp.bfloat16),
        ),
        in_specs=[smem, vmem, vmem, anywhere],
        out_specs=(vmem,) * 2,
        compiler_params=PARAMS,
        cost_estimate=cost(0, 16 * rows * width),
    )(place, tokens, mate, column)

    owned, wide = frag_outer.shape
    block = jax.ShapeDtypeStruct((spots * owned, wide), jnp.bfloat16)
    parts = pl.pallas_call(
        sort_kernel,
        out_shape=(block,) * ZL,
        in_specs=[smem, vmem, anywhere],
        out_specs=(vmem,) * ZL,
        scratch_shapes=[pltpu.VMEM((ZL,) + block.shape, block.dtype)],
        compiler_params=PARAMS,
    )(place, frag_local, column)
    parts = [lax.ppermute(p, "zl", [(i, i ^ j) for i in range(ZL)]) if j else p for j, p in enumerate(parts)]
    part = pl.pallas_call(
        reduce_kernel,
        out_shape=jax.ShapeDtypeStruct(block.shape, jnp.float32),
        in_specs=[vmem] * ZL,
        out_specs=vmem,
        compiler_params=PARAMS,
    )(*parts)

    err = pl.pallas_call(
        error_kernel,
        out_shape=jax.ShapeDtypeStruct((2 * rows, half), jnp.bfloat16),
        in_specs=[smem] + [vmem] * 4,
        out_specs=vmem,
        compiler_params=PARAMS,
        cost_estimate=cost(4 * rows * width * half, 8 * rows * width),
    )(place, both, key, targets, goal_mate)
    err_mate = lax.ppermute(err, "c", SWAP)
    rate = INNER_RATE / width
    short = jax.ShapeDtypeStruct((own_rows // 2, columns), jnp.bfloat16)
    long = jax.ShapeDtypeStruct((own_rows, columns), jnp.bfloat16)
    full = jax.ShapeDtypeStruct((own_rows, columns), jnp.float32)
    out_up, out_down = pl.pallas_call(
        far_kernel,
        out_shape=(short,) * 2,
        in_specs=[smem] + [vmem] * 3 + [anywhere],
        out_specs=(vmem,) * 2,
        compiler_params=PARAMS,
    )(place, xt, err, err_mate, part)

    far_up = shift(out_up, 1)
    far_down = shift(out_down, -1)
    up, down, base, part = pl.pallas_call(
        functools.partial(near_kernel, rate=rate),
        out_shape=(full,) * 3 + (jax.ShapeDtypeStruct(part.shape, part.dtype),),
        in_specs=[smem] + [vmem] * 5 + [anywhere],
        out_specs=(vmem,) * 4,
        compiler_params=PARAMS,
    )(place, xt, err, err_mate, w_key, part, out_up)

    def passed(part, far, half):
        return pl.pallas_call(
            functools.partial(pass_kernel, half=half),
            out_shape=long,
            in_specs=[vmem] * 2,
            out_specs=vmem,
            compiler_params=PARAMS,
        )(part, far)

    up = shift(passed(up, far_up, 0), 1)
    down = shift(passed(down, far_down, 1), -1)
    new_key = pl.pallas_call(
        functools.partial(finish_kernel, rate=rate),
        out_shape=full,
        in_specs=[vmem] * 3,
        out_specs=vmem,
        compiler_params=PARAMS,
    )(base, up, down)
    part = lax.all_to_all(part.reshape(spots, owned, wide), ("x", "y"), 0, 0, tiled=True)
    mean = frag_outer - part.sum(0) / (spots * ZL)
    new_moment = MOMENTUM * frag_moment + mean
    new_outer = frag_outer - OUTER_RATE * (mean + MOMENTUM * new_moment)
    return (new_key, new_outer, new_moment)


def solution(mesh):
    grid = Mesh(mesh.devices.reshape(X, Y, ZL, ZH, 2), ("x", "y", "zl", "zh", "c"))
    replica, fsdp = ("x", "y", "zl"), ("zh", "c")
    in_specs = (
        P(replica + fsdp, None),
        P(fsdp, None),
        P(replica + fsdp, None),
        P(fsdp + replica, None),
        P(replica + fsdp, None),
        P(fsdp + replica, None),
    )
    out_specs = (
        P(replica + fsdp, None),
        P(fsdp + replica, None),
        P(fsdp + replica, None),
    )
    return jax.shard_map(
        on_device, mesh=grid, in_specs=in_specs, out_specs=out_specs, check_vma=False
    )
```

```python
import functools

import jax
import jax.numpy as jnp
from jax import lax
from jax.experimental import pallas as pl
from jax.experimental.pallas import tpu as pltpu
from jax.sharding import Mesh, PartitionSpec as P

INNER_RATE = 4.0
OUTER_RATE = 0.7
MOMENTUM = 0.9

X, Y, ZL, ZH = 4, 4, 4, 4
PARAMS = pltpu.CompilerParams(vmem_limit_bytes=16 * 1024 * 1024)
SWAP = [(0, 1), (1, 0)]


def cost(flops, touched):
    return pl.CostEstimate(flops=flops, bytes_accessed=touched, transcendentals=0)


def round_z(a, cross):
    pairs = []
    for zh in range(ZH):
        for core in range(2):
            there = (zh + 1 - 2 * core) % ZH
            pairs.append((zh * 2 + core, there * 2 + (core ^ cross)))
    return lax.ppermute(a, ("zh", "c"), pairs)


def transpose_kernel(place, own, mate, order, out, both):
    del order
    zh, core = place[0], place[1]
    other = 1 - core
    width = out.shape[1]
    tokens = own.shape[0]
    both[:tokens] = own[...]
    both[tokens:] = mate[...]
    far = lax.rem(zh + 2, ZH)
    near = lax.rem(zh + 1 + 2 * core, ZH)
    for j, (chip, block, half) in enumerate(
        (
            (far, core, core),
            (far, other, core),
            (near, core, core),
            (near, core, other),
            (near, other, core),
            (near, other, other),
            (zh, core, 0),
            (zh, core, 1),
        )
    ):
        columns = pl.ds(pl.multiple_of(((chip * 2 + block) * 2 + half) * width, width), width)
        out[j, :, :tokens] = own[:, columns].T
        out[j, :, tokens:] = mate[:, columns].T


def spread_kernel(place, column, out):
    width = out.shape[3]
    at = place[1] * width
    part = column[:, pl.ds(pl.multiple_of(at, width), width)].reshape(out.shape[1:])
    for i in range(out.shape[0]):
        out[i] = part


def error_kernel(place, both, w, goal_own, goal_mate, out):
    shards, depth = w.shape[1], w.shape[0] * w.shape[2]
    tokens = goal_own.shape[0]
    width = w.shape[3]
    columns = pl.ds(pl.multiple_of(place[1] * width, width), width)
    for i, goal in enumerate((goal_own, goal_mate)):
        at = slice(i * tokens, (i + 1) * tokens)
        keys = jnp.zeros((tokens, width), jnp.float32)
        for f in range(shards):
            keys += jnp.dot(
                both[at, f * depth : (f + 1) * depth],
                w[:, f].reshape(depth, width),
                preferred_element_type=jnp.float32,
            )
        errors = keys - goal[:, columns].astype(jnp.float32)
        out[at, :] = errors.astype(jnp.bfloat16)


def errors_of(place, err_own, err_mate):
    tokens = err_own.shape[0] // 2
    mine = err_own[...]
    other = jnp.concatenate([err_mate[tokens:, :], err_mate[:tokens, :]], axis=0)
    low = jnp.where(place[1] == 0, mine, other)
    high = jnp.where(place[1] == 0, other, mine)
    return jnp.concatenate([low, high], axis=1)


def far_kernel(place, xt, err_own, err_mate, order, *outs):
    del order
    errors = errors_of(place, err_own, err_mate)
    for i, out in enumerate(outs):
        out[...] = jnp.dot(xt[i], errors, preferred_element_type=jnp.float32).astype(out.dtype)


def near_kernel(place, xt, err_own, err_mate, w, part, order, via_a, near_a, via_b, near_b, base, same, *, rate):
    del order
    same[...] = part[...]
    errors = errors_of(place, err_own, err_mate)
    for i, out in enumerate((via_a, near_a, via_b, near_b)):
        out[...] = jnp.dot(xt[2 + i], errors, preferred_element_type=jnp.float32).astype(out.dtype)
    rows = xt.shape[1]
    for h in range(2):
        at = slice(h * rows, (h + 1) * rows)
        base[at, :] = w[at, :] - rate * jnp.dot(xt[6 + h], errors, preferred_element_type=jnp.float32)


def pass_kernel(via, near, far, out):
    rows = far.shape[0]
    out[:rows] = (via[...] + far[...].astype(jnp.float32)).astype(out.dtype)
    out[rows:] = near[...]


def finish_kernel(place, base, straight, crossed, out, *, rate):
    rows = base.shape[0] // 2
    for h in range(2):
        first = place[1] ^ h
        at = slice(h * rows, (h + 1) * rows)
        grad = straight[pl.ds(pl.multiple_of(first * rows, rows), rows), :].astype(jnp.float32)
        grad += crossed[pl.ds(pl.multiple_of((1 - first) * rows, rows), rows), :].astype(jnp.float32)
        out[at, :] = base[at, :] - rate * grad


def sort_kernel(place, given, order, keep, one, two, three, held):
    del order
    spread, rows, wide = held.shape
    owned = given.shape[0] // (spread * X * Y)
    for at in range(0, rows, 2 * owned):
        block = given[at * spread : (at + 2 * owned) * spread].astype(jnp.float32)
        block = block.reshape(2, spread, owned, wide)
        for i in range(spread):
            held[i, at : at + 2 * owned] = block[:, i].reshape(2 * owned, wide).astype(held.dtype)
    for j, out in enumerate((keep, one, two, three)):
        out[...] = held[place[2] ^ j]


def reduce_kernel(keep, one, two, three, out):
    out[...] = (keep[...].astype(jnp.float32) + one[...].astype(jnp.float32)) + (
        two[...].astype(jnp.float32) + three[...].astype(jnp.float32)
    )


def on_device(tokens, w_key, targets, frag_outer, frag_local, frag_moment):
    rows, width = tokens.shape
    own_rows, columns = w_key.shape
    half = columns // 2
    spots = X * Y
    core = lax.axis_index("c")
    zh = lax.axis_index("zh")
    spot = lax.axis_index("x") * Y + lax.axis_index("y")
    place = jnp.stack([zh, core, lax.axis_index("zl")]).astype(jnp.int32)
    smem = pl.BlockSpec(memory_space=pltpu.SMEM)
    vmem = pl.BlockSpec(memory_space=pltpu.VMEM)
    anywhere = pl.BlockSpec(memory_space=pl.ANY)

    piece = own_rows // spots
    mine = lax.dynamic_slice_in_dim(w_key, spot * piece, piece, 0).astype(jnp.bfloat16)
    column = lax.all_gather(mine, ("zh", "c"), axis=0, tiled=True)
    copies = pl.pallas_call(
        spread_kernel,
        out_shape=jax.ShapeDtypeStruct((spots, ZH * 2, piece, half), jnp.bfloat16),
        in_specs=[smem, vmem],
        out_specs=vmem,
        compiler_params=PARAMS,
    )(place, column)
    key = lax.all_to_all(copies, ("x", "y"), 0, 0, tiled=True)

    mate = lax.ppermute(tokens, "c", SWAP)
    goal_mate = lax.ppermute(targets, "c", SWAP)
    xt, both = pl.pallas_call(
        transpose_kernel,
        out_shape=(
            jax.ShapeDtypeStruct((2 * ZH, own_rows // 2, 2 * rows), jnp.bfloat16),
            jax.ShapeDtypeStruct((2 * rows, width), jnp.bfloat16),
        ),
        in_specs=[smem, vmem, vmem, anywhere],
        out_specs=(vmem,) * 2,
        compiler_params=PARAMS,
        cost_estimate=cost(0, 16 * rows * width),
    )(place, tokens, mate, column)

    owned, wide = frag_outer.shape
    block = jax.ShapeDtypeStruct((spots * owned, wide), jnp.bfloat16)
    parts = pl.pallas_call(
        sort_kernel,
        out_shape=(block,) * ZL,
        in_specs=[smem, vmem, anywhere],
        out_specs=(vmem,) * ZL,
        scratch_shapes=[pltpu.VMEM((ZL,) + block.shape, block.dtype)],
        compiler_params=PARAMS,
    )(place, frag_local, column)
    parts = [lax.ppermute(p, "zl", [(i, i ^ j) for i in range(ZL)]) if j else p for j, p in enumerate(parts)]
    part = pl.pallas_call(
        reduce_kernel,
        out_shape=jax.ShapeDtypeStruct(block.shape, jnp.float32),
        in_specs=[vmem] * ZL,
        out_specs=vmem,
        compiler_params=PARAMS,
    )(*parts)

    err = pl.pallas_call(
        error_kernel,
        out_shape=jax.ShapeDtypeStruct((2 * rows, half), jnp.bfloat16),
        in_specs=[smem] + [vmem] * 4,
        out_specs=vmem,
        compiler_params=PARAMS,
        cost_estimate=cost(4 * rows * width * half, 8 * rows * width),
    )(place, both, key, targets, goal_mate)
    err_mate = lax.ppermute(err, "c", SWAP)
    rate = INNER_RATE / width
    short = jax.ShapeDtypeStruct((own_rows // 2, columns), jnp.bfloat16)
    middle = jax.ShapeDtypeStruct((own_rows // 2, columns), jnp.float32)
    long = jax.ShapeDtypeStruct((own_rows, columns), jnp.bfloat16)
    full = jax.ShapeDtypeStruct((own_rows, columns), jnp.float32)
    out_a, out_b = pl.pallas_call(
        far_kernel,
        out_shape=(short,) * 2,
        in_specs=[smem] + [vmem] * 3 + [anywhere],
        out_specs=(vmem,) * 2,
        compiler_params=PARAMS,
    )(place, xt, err, err_mate, part)

    far_a = round_z(out_a, 0)
    far_b = round_z(out_b, 0)
    via_a, near_a, via_b, near_b, base, part = pl.pallas_call(
        functools.partial(near_kernel, rate=rate),
        out_shape=(middle, short, middle, short, full, jax.ShapeDtypeStruct(part.shape, part.dtype)),
        in_specs=[smem] + [vmem] * 5 + [anywhere],
        out_specs=(vmem,) * 6,
        compiler_params=PARAMS,
    )(place, xt, err, err_mate, w_key, part, out_a)

    def passed(via, near, far):
        return pl.pallas_call(
            pass_kernel,
            out_shape=long,
            in_specs=[vmem] * 3,
            out_specs=vmem,
            compiler_params=PARAMS,
        )(via, near, far)

    straight = round_z(passed(via_a, near_a, far_a), 0)
    crossed = round_z(passed(via_b, near_b, far_b), 1)
    new_key = pl.pallas_call(
        functools.partial(finish_kernel, rate=rate),
        out_shape=full,
        in_specs=[smem] + [vmem] * 3,
        out_specs=vmem,
        compiler_params=PARAMS,
    )(place, base, straight, crossed)

    part = lax.all_to_all(part.reshape(spots, owned, wide), ("x", "y"), 0, 0, tiled=True)
    mean = frag_outer - part.sum(0) / (spots * ZL)
    new_moment = MOMENTUM * frag_moment + mean
    new_outer = frag_outer - OUTER_RATE * (mean + MOMENTUM * new_moment)
    return (new_key, new_outer, new_moment)


def solution(mesh):
    grid = Mesh(mesh.devices.reshape(X, Y, ZL, ZH, 2), ("x", "y", "zl", "zh", "c"))
    replica, fsdp = ("x", "y", "zl"), ("zh", "c")
    in_specs = (
        P(replica + fsdp, None),
        P(fsdp, None),
        P(replica + fsdp, None),
        P(fsdp + replica, None),
        P(replica + fsdp, None),
        P(fsdp + replica, None),
    )
    out_specs = (
        P(replica + fsdp, None),
        P(fsdp + replica, None),
        P(fsdp + replica, None),
    )
    return jax.shard_map(
        on_device, mesh=grid, in_specs=in_specs, out_specs=out_specs, check_vma=False
    )
```

```python
import functools

import jax
import jax.numpy as jnp
from jax import lax
from jax.experimental import pallas as pl
from jax.experimental.pallas import tpu as pltpu
from jax.sharding import Mesh, PartitionSpec as P

INNER_RATE = 4.0
OUTER_RATE = 0.7
MOMENTUM = 0.9

X, Y, ZL, ZH = 4, 4, 4, 4
PARAMS = pltpu.CompilerParams(vmem_limit_bytes=16 * 1024 * 1024)
SWAP = [(0, 1), (1, 0)]


def cost(flops, touched):
    return pl.CostEstimate(flops=flops, bytes_accessed=touched, transcendentals=0)


def round_z(a, cross):
    pairs = []
    for zh in range(ZH):
        for core in range(2):
            there = (zh + 1 - 2 * core) % ZH
            pairs.append((zh * 2 + core, there * 2 + (core ^ cross)))
    return lax.ppermute(a, ("zh", "c"), pairs)


def transpose_kernel(place, own, targets, mate, goal, order, far_xt, near_xt, own_xt, both):
    del order
    zh, core = place[0], place[1]
    other = 1 - core
    width = far_xt.shape[1]
    tokens, deep = own.shape
    half = targets.shape[1] // 2
    both[:tokens, :deep] = own[...]
    both[tokens:, :deep] = mate[...]
    columns = pl.ds(pl.multiple_of(core * half, half), half)
    both[:tokens, deep:] = targets[:, columns]
    both[tokens:, deep:] = goal[:, columns]
    far = lax.rem(zh + 2, ZH)
    near = lax.rem(zh + 1 + 2 * core, ZH)
    for out, places in (
        (far_xt, ((far, core, core), (far, other, core))),
        (near_xt, ((near, core, core), (near, core, other), (near, other, core), (near, other, other))),
        (own_xt, ((zh, core, 0), (zh, core, 1))),
    ):
        for j, (chip, block, half) in enumerate(places):
            columns = pl.ds(pl.multiple_of(((chip * 2 + block) * 2 + half) * width, width), width)
            out[j, :, :tokens] = own[:, columns].T
            out[j, :, tokens:] = mate[:, columns].T


def spread_kernel(place, column, out):
    width = out.shape[3]
    at = place[1] * width
    part = column[:, pl.ds(pl.multiple_of(at, width), width)].reshape(out.shape[1:])
    for i in range(out.shape[0]):
        out[i] = part


def error_kernel(both, w, out):
    shards, depth = w.shape[1], w.shape[0] * w.shape[2]
    tokens = both.shape[0] // 2
    width = w.shape[3]
    for i in range(2):
        at = slice(i * tokens, (i + 1) * tokens)
        keys = jnp.zeros((tokens, width), jnp.float32)
        for f in range(shards):
            keys += jnp.dot(
                both[at, f * depth : (f + 1) * depth],
                w[:, f].reshape(depth, width),
                preferred_element_type=jnp.float32,
            )
        errors = keys - both[at, shards * depth :].astype(jnp.float32)
        out[at, :] = errors.astype(jnp.bfloat16)


def errors_of(place, err_own, err_mate):
    tokens = err_own.shape[0] // 2
    mine = err_own[...]
    other = jnp.concatenate([err_mate[tokens:, :], err_mate[:tokens, :]], axis=0)
    low = jnp.where(place[1] == 0, mine, other)
    high = jnp.where(place[1] == 0, other, mine)
    return jnp.concatenate([low, high], axis=1)


def far_kernel(place, xt, err_own, err_mate, order, *outs):
    del order
    errors = errors_of(place, err_own, err_mate)
    for i, out in enumerate(outs):
        out[...] = jnp.dot(xt[i], errors, preferred_element_type=jnp.float32).astype(out.dtype)


def near_kernel(place, xt, own_xt, err_own, err_mate, w, part, order, via_a, near_a, via_b, near_b, base, same, *, rate):
    del order
    same[...] = part[...]
    errors = errors_of(place, err_own, err_mate)
    for i, out in enumerate((via_a, near_a, via_b, near_b)):
        out[...] = jnp.dot(xt[i], errors, preferred_element_type=jnp.float32).astype(out.dtype)
    rows = xt.shape[1]
    for h in range(2):
        at = slice(h * rows, (h + 1) * rows)
        base[at, :] = w[at, :] - rate * jnp.dot(own_xt[h], errors, preferred_element_type=jnp.float32)


def pass_kernel(via, near, far, out):
    rows = far.shape[0]
    out[:rows] = (via[...] + far[...].astype(jnp.float32)).astype(out.dtype)
    out[rows:] = near[...]


def finish_kernel(place, base, straight, crossed, out, *, rate):
    rows = base.shape[0] // 2
    for h in range(2):
        first = place[1] ^ h
        at = slice(h * rows, (h + 1) * rows)
        grad = straight[pl.ds(pl.multiple_of(first * rows, rows), rows), :].astype(jnp.float32)
        grad += crossed[pl.ds(pl.multiple_of((1 - first) * rows, rows), rows), :].astype(jnp.float32)
        out[at, :] = base[at, :] - rate * grad


def sort_kernel(place, given, order, keep, one, two, three, held):
    del order
    spread, rows, wide = held.shape
    owned = given.shape[0] // (spread * X * Y)
    for at in range(0, rows, 2 * owned):
        block = given[at * spread : (at + 2 * owned) * spread].astype(jnp.float32)
        block = block.reshape(2, spread, owned, wide)
        for i in range(spread):
            held[i, at : at + 2 * owned] = block[:, i].reshape(2 * owned, wide).astype(held.dtype)
    for j, out in enumerate((keep, one, two, three)):
        out[...] = held[place[2] ^ j]


def reduce_kernel(keep, one, two, three, out):
    out[...] = (keep[...].astype(jnp.float32) + one[...].astype(jnp.float32)) + (
        two[...].astype(jnp.float32) + three[...].astype(jnp.float32)
    )


def on_device(tokens, w_key, targets, frag_outer, frag_local, frag_moment):
    rows, width = tokens.shape
    own_rows, columns = w_key.shape
    half = columns // 2
    spots = X * Y
    core = lax.axis_index("c")
    zh = lax.axis_index("zh")
    spot = lax.axis_index("x") * Y + lax.axis_index("y")
    place = jnp.stack([zh, core, lax.axis_index("zl")]).astype(jnp.int32)
    smem = pl.BlockSpec(memory_space=pltpu.SMEM)
    vmem = pl.BlockSpec(memory_space=pltpu.VMEM)
    anywhere = pl.BlockSpec(memory_space=pl.ANY)

    piece = own_rows // spots
    mine = lax.dynamic_slice_in_dim(w_key, spot * piece, piece, 0).astype(jnp.bfloat16)
    column = lax.all_gather(mine, ("zh", "c"), axis=0, tiled=True)
    copies = pl.pallas_call(
        spread_kernel,
        out_shape=jax.ShapeDtypeStruct((spots, ZH * 2, piece, half), jnp.bfloat16),
        in_specs=[smem, vmem],
        out_specs=vmem,
        compiler_params=PARAMS,
    )(place, column)
    key = lax.all_to_all(copies, ("x", "y"), 0, 0, tiled=True)

    mate = lax.ppermute(tokens, "c", SWAP)
    goal = lax.ppermute(targets, "c", SWAP)

    def turned(pieces):
        return jax.ShapeDtypeStruct((pieces, own_rows // 2, 2 * rows), jnp.bfloat16)

    far_xt, near_xt, own_xt, both = pl.pallas_call(
        transpose_kernel,
        out_shape=(turned(2), turned(4), turned(2), jax.ShapeDtypeStruct((2 * rows, width + half), jnp.bfloat16)),
        in_specs=[smem] + [vmem] * 4 + [anywhere],
        out_specs=(vmem,) * 4,
        compiler_params=PARAMS,
        cost_estimate=cost(0, 16 * rows * width),
    )(place, tokens, targets, mate, goal, column)

    owned, wide = frag_outer.shape
    block = jax.ShapeDtypeStruct((spots * owned, wide), jnp.bfloat16)
    parts = pl.pallas_call(
        sort_kernel,
        out_shape=(block,) * ZL,
        in_specs=[smem, vmem, anywhere],
        out_specs=(vmem,) * ZL,
        scratch_shapes=[pltpu.VMEM((ZL,) + block.shape, block.dtype)],
        compiler_params=PARAMS,
    )(place, frag_local, column)
    parts = [lax.ppermute(p, "zl", [(i, i ^ j) for i in range(ZL)]) if j else p for j, p in enumerate(parts)]
    part = pl.pallas_call(
        reduce_kernel,
        out_shape=jax.ShapeDtypeStruct(block.shape, jnp.float32),
        in_specs=[vmem] * ZL,
        out_specs=vmem,
        compiler_params=PARAMS,
    )(*parts)

    err = pl.pallas_call(
        error_kernel,
        out_shape=jax.ShapeDtypeStruct((2 * rows, half), jnp.bfloat16),
        in_specs=[vmem] * 2,
        out_specs=vmem,
        compiler_params=PARAMS,
        cost_estimate=cost(4 * rows * width * half, 8 * rows * width),
    )(both, key)
    err_mate = lax.ppermute(err, "c", SWAP)
    rate = INNER_RATE / width
    short = jax.ShapeDtypeStruct((own_rows // 2, columns), jnp.bfloat16)
    middle = jax.ShapeDtypeStruct((own_rows // 2, columns), jnp.float32)
    long = jax.ShapeDtypeStruct((own_rows, columns), jnp.bfloat16)
    full = jax.ShapeDtypeStruct((own_rows, columns), jnp.float32)
    out_a, out_b = pl.pallas_call(
        far_kernel,
        out_shape=(short,) * 2,
        in_specs=[smem] + [vmem] * 3 + [anywhere],
        out_specs=(vmem,) * 2,
        compiler_params=PARAMS,
    )(place, far_xt, err, err_mate, part)

    far_a = round_z(out_a, 0)
    far_b = round_z(out_b, 0)
    via_a, near_a, via_b, near_b, base, part = pl.pallas_call(
        functools.partial(near_kernel, rate=rate),
        out_shape=(middle, short, middle, short, full, jax.ShapeDtypeStruct(part.shape, part.dtype)),
        in_specs=[smem] + [vmem] * 6 + [anywhere],
        out_specs=(vmem,) * 6,
        compiler_params=PARAMS,
    )(place, near_xt, own_xt, err, err_mate, w_key, part, out_a)

    def passed(via, near, far):
        return pl.pallas_call(
            pass_kernel,
            out_shape=long,
            in_specs=[vmem] * 3,
            out_specs=vmem,
            compiler_params=PARAMS,
        )(via, near, far)

    straight = round_z(passed(via_a, near_a, far_a), 0)
    crossed = round_z(passed(via_b, near_b, far_b), 1)
    new_key = pl.pallas_call(
        functools.partial(finish_kernel, rate=rate),
        out_shape=full,
        in_specs=[smem] + [vmem] * 3,
        out_specs=vmem,
        compiler_params=PARAMS,
    )(place, base, straight, crossed)

    part = lax.all_to_all(part.reshape(spots, owned, wide), ("x", "y"), 0, 0, tiled=True)
    mean = frag_outer - part.sum(0) / (spots * ZL)
    new_moment = MOMENTUM * frag_moment + mean
    new_outer = frag_outer - OUTER_RATE * (mean + MOMENTUM * new_moment)
    return (new_key, new_outer, new_moment)


def solution(mesh):
    grid = Mesh(mesh.devices.reshape(X, Y, ZL, ZH, 2), ("x", "y", "zl", "zh", "c"))
    replica, fsdp = ("x", "y", "zl"), ("zh", "c")
    in_specs = (
        P(replica + fsdp, None),
        P(fsdp, None),
        P(replica + fsdp, None),
        P(fsdp + replica, None),
        P(replica + fsdp, None),
        P(fsdp + replica, None),
    )
    out_specs = (
        P(replica + fsdp, None),
        P(fsdp + replica, None),
        P(fsdp + replica, None),
    )
    return jax.shard_map(
        on_device, mesh=grid, in_specs=in_specs, out_specs=out_specs, check_vma=False
    )
```

```python
import functools

import jax
import jax.numpy as jnp
from jax import lax
from jax.experimental import pallas as pl
from jax.experimental.pallas import tpu as pltpu
from jax.sharding import Mesh, PartitionSpec as P

INNER_RATE = 4.0
OUTER_RATE = 0.7
MOMENTUM = 0.9

X, Y, ZL, ZH = 4, 4, 4, 4
PARAMS = pltpu.CompilerParams(vmem_limit_bytes=16 * 1024 * 1024)
SWAP = [(0, 1), (1, 0)]


def cost(flops, touched):
    return pl.CostEstimate(flops=flops, bytes_accessed=touched, transcendentals=0)


def round_z(a, cross):
    pairs = []
    for zh in range(ZH):
        for core in range(2):
            there = (zh + 1 - 2 * core) % ZH
            pairs.append((zh * 2 + core, there * 2 + (core ^ cross)))
    return lax.ppermute(a, ("zh", "c"), pairs)


def transpose_kernel(place, own, targets, mate, goal, order, far_xt, near_xt, own_xt, both):
    del order
    zh, core = place[0], place[1]
    other = 1 - core
    width = far_xt.shape[1]
    tokens, deep = own.shape
    half = targets.shape[1] // 2
    both[:tokens, :deep] = own[...]
    both[tokens:, :deep] = mate[...]
    columns = pl.ds(pl.multiple_of(core * half, half), half)
    both[:tokens, deep:] = targets[:, columns]
    both[tokens:, deep:] = goal[:, columns]
    far = lax.rem(zh + 2, ZH)
    near = lax.rem(zh + 1 + 2 * core, ZH)
    for out, places in (
        (far_xt, ((far, core, core), (far, other, core))),
        (near_xt, ((near, core, core), (near, core, other), (near, other, core), (near, other, other))),
        (own_xt, ((zh, core, 0), (zh, core, 1))),
    ):
        for j, (chip, block, half) in enumerate(places):
            columns = pl.ds(pl.multiple_of(((chip * 2 + block) * 2 + half) * width, width), width)
            out[j, :, :tokens] = own[:, columns].T
            out[j, :, tokens:] = mate[:, columns].T


def spread_kernel(place, column, out):
    width = out.shape[3]
    at = place[1] * width
    part = column[:, pl.ds(pl.multiple_of(at, width), width)].reshape(out.shape[1:])
    for i in range(out.shape[0]):
        out[i] = part


def error_kernel(both, w, out):
    shards, depth = w.shape[1], w.shape[0] * w.shape[2]
    tokens = both.shape[0] // 2
    width = w.shape[3]
    for i in range(2):
        at = slice(i * tokens, (i + 1) * tokens)
        keys = jnp.zeros((tokens, width), jnp.float32)
        for f in range(shards):
            keys += jnp.dot(
                both[at, f * depth : (f + 1) * depth],
                w[:, f].reshape(depth, width),
                preferred_element_type=jnp.float32,
            )
        errors = keys - both[at, shards * depth :].astype(jnp.float32)
        out[at, :] = errors.astype(jnp.bfloat16)


def errors_of(place, err_own, err_mate):
    tokens = err_own.shape[0] // 2
    mine = err_own[...]
    other = jnp.concatenate([err_mate[tokens:, :], err_mate[:tokens, :]], axis=0)
    low = jnp.where(place[1] == 0, mine, other)
    high = jnp.where(place[1] == 0, other, mine)
    return jnp.concatenate([low, high], axis=1)


def far_kernel(place, xt, err_own, err_mate, one, two, three, out):
    del one, two, three
    errors = errors_of(place, err_own, err_mate)
    rows = xt.shape[1]
    for i in range(2):
        part = jnp.dot(xt[i], errors, preferred_element_type=jnp.float32)
        out[i * rows : (i + 1) * rows, :] = part.astype(out.dtype)


def near_kernel(place, xt, own_xt, err_own, err_mate, w, *refs, rate):
    parts, (_, via_a, near_a, via_b, near_b, base, total) = refs[:ZL], refs[ZL:]
    keep, one, two, three = (p[...].astype(jnp.float32) for p in parts)
    total[...] = (keep + one) + (two + three)
    errors = errors_of(place, err_own, err_mate)
    for i, out in enumerate((via_a, near_a, via_b, near_b)):
        out[...] = jnp.dot(xt[i], errors, preferred_element_type=jnp.float32).astype(out.dtype)
    rows = xt.shape[1]
    for h in range(2):
        at = slice(h * rows, (h + 1) * rows)
        base[at, :] = w[at, :] - rate * jnp.dot(own_xt[h], errors, preferred_element_type=jnp.float32)


def pass_kernel(via, far, out, *, half):
    rows = via.shape[0]
    out[...] = (via[...] + far[half * rows : (half + 1) * rows, :].astype(jnp.float32)).astype(out.dtype)


def finish_kernel(place, base, near_a, near_b, sum_a, sum_b, out, *, rate):
    rows = near_a.shape[0]
    core = place[1]
    for first, (plain, total) in ((True, (near_b, sum_a)), (False, (near_a, sum_b))):
        half = core if first else 1 - core
        at = pl.ds(pl.multiple_of(half * rows, rows), rows)
        grad = plain[...].astype(jnp.float32) + total[...].astype(jnp.float32)
        out[at, :] = base[at, :] - rate * grad


def sort_kernel(place, given, order, keep, one, two, three, held):
    del order
    spread, rows, wide = held.shape
    owned = given.shape[0] // (spread * X * Y)
    for at in range(0, rows, 2 * owned):
        block = given[at * spread : (at + 2 * owned) * spread].astype(jnp.float32)
        block = block.reshape(2, spread, owned, wide)
        for i in range(spread):
            held[i, at : at + 2 * owned] = block[:, i].reshape(2 * owned, wide).astype(held.dtype)
    for j, out in enumerate((keep, one, two, three)):
        out[...] = held[place[2] ^ j]


def on_device(tokens, w_key, targets, frag_outer, frag_local, frag_moment):
    rows, width = tokens.shape
    own_rows, columns = w_key.shape
    half = columns // 2
    spots = X * Y
    core = lax.axis_index("c")
    zh = lax.axis_index("zh")
    spot = lax.axis_index("x") * Y + lax.axis_index("y")
    place = jnp.stack([zh, core, lax.axis_index("zl")]).astype(jnp.int32)
    smem = pl.BlockSpec(memory_space=pltpu.SMEM)
    vmem = pl.BlockSpec(memory_space=pltpu.VMEM)
    anywhere = pl.BlockSpec(memory_space=pl.ANY)

    piece = own_rows // spots
    mine = lax.dynamic_slice_in_dim(w_key, spot * piece, piece, 0).astype(jnp.bfloat16)
    column = lax.all_gather(mine, ("zh", "c"), axis=0, tiled=True)
    copies = pl.pallas_call(
        spread_kernel,
        out_shape=jax.ShapeDtypeStruct((spots, ZH * 2, piece, half), jnp.bfloat16),
        in_specs=[smem, vmem],
        out_specs=vmem,
        compiler_params=PARAMS,
    )(place, column)
    key = lax.all_to_all(copies, ("x", "y"), 0, 0, tiled=True)

    mate = lax.ppermute(tokens, "c", SWAP)
    goal = lax.ppermute(targets, "c", SWAP)

    def turned(pieces):
        return jax.ShapeDtypeStruct((pieces, own_rows // 2, 2 * rows), jnp.bfloat16)

    far_xt, near_xt, own_xt, both = pl.pallas_call(
        transpose_kernel,
        out_shape=(turned(2), turned(4), turned(2), jax.ShapeDtypeStruct((2 * rows, width + half), jnp.bfloat16)),
        in_specs=[smem] + [vmem] * 4 + [anywhere],
        out_specs=(vmem,) * 4,
        compiler_params=PARAMS,
        cost_estimate=cost(0, 16 * rows * width),
    )(place, tokens, targets, mate, goal, column)

    owned, wide = frag_outer.shape
    block = jax.ShapeDtypeStruct((spots * owned, wide), jnp.bfloat16)
    parts = pl.pallas_call(
        sort_kernel,
        out_shape=(block,) * ZL,
        in_specs=[smem, vmem, anywhere],
        out_specs=(vmem,) * ZL,
        scratch_shapes=[pltpu.VMEM((ZL,) + block.shape, block.dtype)],
        compiler_params=PARAMS,
    )(place, frag_local, column)
    parts = [lax.ppermute(p, "zl", [(i, i ^ j) for i in range(ZL)]) if j else p for j, p in enumerate(parts)]
    err = pl.pallas_call(
        error_kernel,
        out_shape=jax.ShapeDtypeStruct((2 * rows, half), jnp.bfloat16),
        in_specs=[vmem] * 2,
        out_specs=vmem,
        compiler_params=PARAMS,
        cost_estimate=cost(4 * rows * width * half, 8 * rows * width),
    )(both, key)
    err_mate = lax.ppermute(err, "c", SWAP)
    rate = INNER_RATE / width
    short = jax.ShapeDtypeStruct((own_rows // 2, columns), jnp.bfloat16)
    middle = jax.ShapeDtypeStruct((own_rows // 2, columns), jnp.float32)
    long = jax.ShapeDtypeStruct((own_rows, columns), jnp.bfloat16)
    full = jax.ShapeDtypeStruct((own_rows, columns), jnp.float32)
    out = pl.pallas_call(
        far_kernel,
        out_shape=long,
        in_specs=[smem] + [vmem] * 3 + [anywhere] * 3,
        out_specs=vmem,
        compiler_params=PARAMS,
    )(place, far_xt, err, err_mate, *parts[1:])

    far = round_z(out, 0)
    via_a, near_a, via_b, near_b, base, part = pl.pallas_call(
        functools.partial(near_kernel, rate=rate),
        out_shape=(middle, short, middle, short, full, jax.ShapeDtypeStruct(block.shape, jnp.float32)),
        in_specs=[smem] + [vmem] * (5 + ZL) + [anywhere],
        out_specs=(vmem,) * 6,
        compiler_params=PARAMS,
    )(place, near_xt, own_xt, err, err_mate, w_key, *parts, out)
    near_a = round_z(near_a, 0)
    near_b = round_z(near_b, 1)

    def passed(via, half):
        return pl.pallas_call(
            functools.partial(pass_kernel, half=half),
            out_shape=short,
            in_specs=[vmem] * 2,
            out_specs=vmem,
            compiler_params=PARAMS,
        )(via, far)

    sum_a = round_z(passed(via_a, 0), 0)
    sum_b = round_z(passed(via_b, 1), 1)
    new_key = pl.pallas_call(
        functools.partial(finish_kernel, rate=rate),
        out_shape=full,
        in_specs=[smem] + [vmem] * 5,
        out_specs=vmem,
        compiler_params=PARAMS,
    )(place, base, near_a, near_b, sum_a, sum_b)

    part = lax.all_to_all(part.reshape(spots, owned, wide), ("x", "y"), 0, 0, tiled=True)
    mean = frag_outer - part.sum(0) / (spots * ZL)
    new_moment = MOMENTUM * frag_moment + mean
    new_outer = frag_outer - OUTER_RATE * (mean + MOMENTUM * new_moment)
    return (new_key, new_outer, new_moment)


def solution(mesh):
    grid = Mesh(mesh.devices.reshape(X, Y, ZL, ZH, 2), ("x", "y", "zl", "zh", "c"))
    replica, fsdp = ("x", "y", "zl"), ("zh", "c")
    in_specs = (
        P(replica + fsdp, None),
        P(fsdp, None),
        P(replica + fsdp, None),
        P(fsdp + replica, None),
        P(replica + fsdp, None),
        P(fsdp + replica, None),
    )
    out_specs = (
        P(replica + fsdp, None),
        P(fsdp + replica, None),
        P(fsdp + replica, None),
    )
    return jax.shard_map(
        on_device, mesh=grid, in_specs=in_specs, out_specs=out_specs, check_vma=False
    )
```

```python
import functools

import jax
import jax.numpy as jnp
from jax import lax
from jax.experimental import pallas as pl
from jax.experimental.pallas import tpu as pltpu
from jax.sharding import Mesh, PartitionSpec as P

INNER_RATE = 4.0
OUTER_RATE = 0.7
MOMENTUM = 0.9

X, Y, ZL, ZH = 4, 4, 4, 4
PARAMS = pltpu.CompilerParams(vmem_limit_bytes=16 * 1024 * 1024)
SWAP = [(0, 1), (1, 0)]


def cost(flops, touched):
    return pl.CostEstimate(flops=flops, bytes_accessed=touched, transcendentals=0)


def round_z(a, cross):
    pairs = []
    for zh in range(ZH):
        for core in range(2):
            there = (zh + 1 - 2 * core) % ZH
            pairs.append((zh * 2 + core, there * 2 + (core ^ cross)))
    return lax.ppermute(a, ("zh", "c"), pairs)


def transpose_kernel(place, own, targets, mate, goal, order, far_xt, near_xt, own_xt, both):
    del order
    zh, core = place[0], place[1]
    other = 1 - core
    width = far_xt.shape[1]
    tokens, deep = own.shape
    half = targets.shape[1] // 2
    both[:tokens, :deep] = own[...]
    both[tokens:, :deep] = mate[...]
    columns = pl.ds(pl.multiple_of(core * half, half), half)
    both[:tokens, deep:] = targets[:, columns]
    both[tokens:, deep:] = goal[:, columns]
    far = lax.rem(zh + 2, ZH)
    near = lax.rem(zh + 1 + 2 * core, ZH)
    for out, places in (
        (far_xt, ((far, core, core), (far, other, core))),
        (near_xt, ((near, core, core), (near, core, other), (near, other, core), (near, other, other))),
        (own_xt, ((zh, core, 0), (zh, core, 1))),
    ):
        for j, (chip, block, half) in enumerate(places):
            columns = pl.ds(pl.multiple_of(((chip * 2 + block) * 2 + half) * width, width), width)
            out[j, :, :tokens] = own[:, columns].T
            out[j, :, tokens:] = mate[:, columns].T


def error_kernel(both, w, out):
    shards, depth = w.shape[1], w.shape[0] * w.shape[2]
    tokens = both.shape[0] // 2
    width = w.shape[3]
    for i in range(2):
        at = slice(i * tokens, (i + 1) * tokens)
        keys = jnp.zeros((tokens, width), jnp.float32)
        for f in range(shards):
            keys += jnp.dot(
                both[at, f * depth : (f + 1) * depth],
                w[:, f].reshape(depth, width),
                preferred_element_type=jnp.float32,
            )
        errors = keys - both[at, shards * depth :].astype(jnp.float32)
        out[at, :] = errors.astype(jnp.bfloat16)


def errors_of(place, err_own, err_mate):
    tokens = err_own.shape[0] // 2
    mine = err_own[...]
    other = jnp.concatenate([err_mate[tokens:, :], err_mate[:tokens, :]], axis=0)
    low = jnp.where(place[1] == 0, mine, other)
    high = jnp.where(place[1] == 0, other, mine)
    return jnp.concatenate([low, high], axis=1)


def far_kernel(place, xt, err_own, err_mate, one, two, three, out):
    del one, two, three
    errors = errors_of(place, err_own, err_mate)
    rows = xt.shape[1]
    for i in range(2):
        part = jnp.dot(xt[i], errors, preferred_element_type=jnp.float32)
        out[i * rows : (i + 1) * rows, :] = part.astype(out.dtype)


def near_kernel(place, xt, own_xt, err_own, err_mate, w, *refs, rate):
    parts, (_, via_a, near_a, via_b, near_b, base, total) = refs[:ZL], refs[ZL:]
    keep, one, two, three = (p[...].astype(jnp.float32) for p in parts)
    total[...] = (keep + one) + (two + three)
    errors = errors_of(place, err_own, err_mate)
    for i, out in enumerate((via_a, near_a, via_b, near_b)):
        out[...] = jnp.dot(xt[i], errors, preferred_element_type=jnp.float32).astype(out.dtype)
    rows = xt.shape[1]
    for h in range(2):
        at = slice(h * rows, (h + 1) * rows)
        base[at, :] = w[at, :] - rate * jnp.dot(own_xt[h], errors, preferred_element_type=jnp.float32)


def pass_kernel(via, far, out, *, half):
    rows = via.shape[0]
    out[...] = (via[...] + far[half * rows : (half + 1) * rows, :].astype(jnp.float32)).astype(out.dtype)


def fold_kernel(place, base, near_a, near_b, out, *, rate):
    rows = near_a.shape[0]
    for half, near in ((place[1], near_b), (1 - place[1], near_a)):
        at = pl.ds(pl.multiple_of(half * rows, rows), rows)
        out[at, :] = base[at, :] - rate * near[...].astype(jnp.float32)


def finish_kernel(place, base, sum_a, sum_b, out, *, rate):
    rows = sum_a.shape[0]
    for half, total in ((place[1], sum_a), (1 - place[1], sum_b)):
        at = pl.ds(pl.multiple_of(half * rows, rows), rows)
        out[at, :] = base[at, :] - rate * total[...].astype(jnp.float32)


def sort_kernel(place, given, order, keep, one, two, three, held):
    del order
    spread, rows, wide = held.shape
    owned = given.shape[0] // (spread * X * Y)
    for at in range(0, rows, 2 * owned):
        block = given[at * spread : (at + 2 * owned) * spread].astype(jnp.float32)
        block = block.reshape(2, spread, owned, wide)
        for i in range(spread):
            held[i, at : at + 2 * owned] = block[:, i].reshape(2 * owned, wide).astype(held.dtype)
    for j, out in enumerate((keep, one, two, three)):
        out[...] = held[place[2] ^ j]


def on_device(tokens, w_key, targets, frag_outer, frag_local, frag_moment):
    rows, width = tokens.shape
    own_rows, columns = w_key.shape
    half = columns // 2
    spots = X * Y
    core = lax.axis_index("c")
    zh = lax.axis_index("zh")
    spot = lax.axis_index("x") * Y + lax.axis_index("y")
    place = jnp.stack([zh, core, lax.axis_index("zl")]).astype(jnp.int32)
    smem = pl.BlockSpec(memory_space=pltpu.SMEM)
    vmem = pl.BlockSpec(memory_space=pltpu.VMEM)
    anywhere = pl.BlockSpec(memory_space=pl.ANY)

    piece = own_rows // spots
    mine = lax.dynamic_slice_in_dim(w_key, spot * piece, piece, 0).astype(jnp.bfloat16)
    column = lax.all_gather(mine, ("zh", "c"), axis=0, tiled=True)
    part = lax.dynamic_slice_in_dim(column, core * half, half, 1).reshape(ZH * 2, piece, half)
    copies = jnp.broadcast_to(part[None], (spots,) + part.shape)
    key = lax.all_to_all(copies, ("x", "y"), 0, 0, tiled=True)

    mate = lax.ppermute(tokens, "c", SWAP)
    goal = lax.ppermute(targets, "c", SWAP)

    def turned(pieces):
        return jax.ShapeDtypeStruct((pieces, own_rows // 2, 2 * rows), jnp.bfloat16)

    far_xt, near_xt, own_xt, both = pl.pallas_call(
        transpose_kernel,
        out_shape=(turned(2), turned(4), turned(2), jax.ShapeDtypeStruct((2 * rows, width + half), jnp.bfloat16)),
        in_specs=[smem] + [vmem] * 4 + [anywhere],
        out_specs=(vmem,) * 4,
        compiler_params=PARAMS,
        cost_estimate=cost(0, 16 * rows * width),
    )(place, tokens, targets, mate, goal, column)

    owned, wide = frag_outer.shape
    block = jax.ShapeDtypeStruct((spots * owned, wide), jnp.bfloat16)
    parts = pl.pallas_call(
        sort_kernel,
        out_shape=(block,) * ZL,
        in_specs=[smem, vmem, anywhere],
        out_specs=(vmem,) * ZL,
        scratch_shapes=[pltpu.VMEM((ZL,) + block.shape, block.dtype)],
        compiler_params=PARAMS,
    )(place, frag_local, column)
    parts = [lax.ppermute(p, "zl", [(i, i ^ j) for i in range(ZL)]) if j else p for j, p in enumerate(parts)]
    err = pl.pallas_call(
        error_kernel,
        out_shape=jax.ShapeDtypeStruct((2 * rows, half), jnp.bfloat16),
        in_specs=[vmem] * 2,
        out_specs=vmem,
        compiler_params=PARAMS,
        cost_estimate=cost(4 * rows * width * half, 8 * rows * width),
    )(both, key)
    err_mate = lax.ppermute(err, "c", SWAP)
    rate = INNER_RATE / width
    short = jax.ShapeDtypeStruct((own_rows // 2, columns), jnp.bfloat16)
    middle = jax.ShapeDtypeStruct((own_rows // 2, columns), jnp.float32)
    long = jax.ShapeDtypeStruct((own_rows, columns), jnp.bfloat16)
    full = jax.ShapeDtypeStruct((own_rows, columns), jnp.float32)
    out = pl.pallas_call(
        far_kernel,
        out_shape=long,
        in_specs=[smem] + [vmem] * 3 + [anywhere] * 3,
        out_specs=vmem,
        compiler_params=PARAMS,
    )(place, far_xt, err, err_mate, *parts[1:])

    far = round_z(out, 0)
    via_a, near_a, via_b, near_b, base, part = pl.pallas_call(
        functools.partial(near_kernel, rate=rate),
        out_shape=(middle, short, middle, short, full, jax.ShapeDtypeStruct(block.shape, jnp.float32)),
        in_specs=[smem] + [vmem] * (5 + ZL) + [anywhere],
        out_specs=(vmem,) * 6,
        compiler_params=PARAMS,
    )(place, near_xt, own_xt, err, err_mate, w_key, *parts, out)
    near_a = round_z(near_a, 0)
    near_b = round_z(near_b, 1)

    def passed(via, half):
        return pl.pallas_call(
            functools.partial(pass_kernel, half=half),
            out_shape=short,
            in_specs=[vmem] * 2,
            out_specs=vmem,
            compiler_params=PARAMS,
        )(via, far)

    sum_a = round_z(passed(via_a, 0), 0)
    sum_b = round_z(passed(via_b, 1), 1)
    base = pl.pallas_call(
        functools.partial(fold_kernel, rate=rate),
        out_shape=full,
        in_specs=[smem] + [vmem] * 3,
        out_specs=vmem,
        compiler_params=PARAMS,
    )(place, base, near_a, near_b)
    new_key = pl.pallas_call(
        functools.partial(finish_kernel, rate=rate),
        out_shape=full,
        in_specs=[smem] + [vmem] * 3,
        out_specs=vmem,
        compiler_params=PARAMS,
    )(place, base, sum_a, sum_b)

    part = lax.all_to_all(part.reshape(spots, owned, wide), ("x", "y"), 0, 0, tiled=True)
    mean = frag_outer - part.sum(0) / (spots * ZL)
    new_moment = MOMENTUM * frag_moment + mean
    new_outer = frag_outer - OUTER_RATE * (mean + MOMENTUM * new_moment)
    return (new_key, new_outer, new_moment)


def solution(mesh):
    grid = Mesh(mesh.devices.reshape(X, Y, ZL, ZH, 2), ("x", "y", "zl", "zh", "c"))
    replica, fsdp = ("x", "y", "zl"), ("zh", "c")
    in_specs = (
        P(replica + fsdp, None),
        P(fsdp, None),
        P(replica + fsdp, None),
        P(fsdp + replica, None),
        P(replica + fsdp, None),
        P(fsdp + replica, None),
    )
    out_specs = (
        P(replica + fsdp, None),
        P(fsdp + replica, None),
        P(fsdp + replica, None),
    )
    return jax.shard_map(
        on_device, mesh=grid, in_specs=in_specs, out_specs=out_specs, check_vma=False
    )
```

```python
import functools

import jax
import jax.numpy as jnp
from jax import lax
from jax.experimental import pallas as pl
from jax.experimental.pallas import tpu as pltpu
from jax.sharding import Mesh, PartitionSpec as P

INNER_RATE = 4.0
OUTER_RATE = 0.7
MOMENTUM = 0.9

X, Y, ZL, ZH = 4, 4, 4, 4
PARAMS = pltpu.CompilerParams(vmem_limit_bytes=16 * 1024 * 1024)
SWAP = [(0, 1), (1, 0)]


def cost(flops, touched):
    return pl.CostEstimate(flops=flops, bytes_accessed=touched, transcendentals=0)


def round_z(a, cross):
    pairs = []
    for zl in range(ZL):
        for zh in range(ZH):
            for core in range(2):
                there = (zh + 1 - 2 * (core ^ (zl & 1))) % ZH
                pairs.append(((zl * ZH + zh) * 2 + core, (zl * ZH + there) * 2 + (core ^ cross)))
    return lax.ppermute(a, ("zl", "zh", "c"), pairs)


def transpose_kernel(place, own, targets, mate, goal, order, far_xt, near_xt, own_xt, both):
    del order
    zh, core = place[0], place[1]
    other = 1 - core
    width = far_xt.shape[1]
    tokens, deep = own.shape
    half = targets.shape[1] // 2
    both[:tokens, :deep] = own[...]
    both[tokens:, :deep] = mate[...]
    columns = pl.ds(pl.multiple_of(core * half, half), half)
    both[:tokens, deep:] = targets[:, columns]
    both[tokens:, deep:] = goal[:, columns]
    far = lax.rem(zh + 2, ZH)
    near = lax.rem(zh + 1 + 2 * (core ^ (place[2] & 1)), ZH)
    for out, places in (
        (far_xt, ((far, core, core), (far, other, core))),
        (near_xt, ((near, core, core), (near, core, other), (near, other, core), (near, other, other))),
        (own_xt, ((zh, core, 0), (zh, core, 1))),
    ):
        for j, (chip, block, half) in enumerate(places):
            columns = pl.ds(pl.multiple_of(((chip * 2 + block) * 2 + half) * width, width), width)
            out[j, :, :tokens] = own[:, columns].T
            out[j, :, tokens:] = mate[:, columns].T


def error_kernel(both, w, out):
    shards, depth = w.shape[1], w.shape[0] * w.shape[2]
    tokens = both.shape[0] // 2
    width = w.shape[3]
    for i in range(2):
        at = slice(i * tokens, (i + 1) * tokens)
        keys = jnp.zeros((tokens, width), jnp.float32)
        for f in range(shards):
            keys += jnp.dot(
                both[at, f * depth : (f + 1) * depth],
                w[:, f].reshape(depth, width),
                preferred_element_type=jnp.float32,
            )
        errors = keys - both[at, shards * depth :].astype(jnp.float32)
        out[at, :] = errors.astype(jnp.bfloat16)


def errors_of(place, err_own, err_mate):
    tokens = err_own.shape[0] // 2
    mine = err_own[...]
    other = jnp.concatenate([err_mate[tokens:, :], err_mate[:tokens, :]], axis=0)
    low = jnp.where(place[1] == 0, mine, other)
    high = jnp.where(place[1] == 0, other, mine)
    return jnp.concatenate([low, high], axis=1)


def far_kernel(place, xt, err_own, err_mate, one, two, three, out):
    del one, two, three
    errors = errors_of(place, err_own, err_mate)
    rows = xt.shape[1]
    for i in range(2):
        part = jnp.dot(xt[i], errors, preferred_element_type=jnp.float32)
        out[i * rows : (i + 1) * rows, :] = part.astype(out.dtype)


def near_kernel(place, xt, own_xt, err_own, err_mate, w, *refs, rate):
    parts, (_, via_a, near_a, via_b, near_b, base, total) = refs[:ZL], refs[ZL:]
    keep, one, two, three = (p[...].astype(jnp.float32) for p in parts)
    total[...] = (keep + one) + (two + three)
    errors = errors_of(place, err_own, err_mate)
    for i, out in enumerate((via_a, near_a, via_b, near_b)):
        out[...] = jnp.dot(xt[i], errors, preferred_element_type=jnp.float32).astype(out.dtype)
    rows = xt.shape[1]
    for h in range(2):
        at = slice(h * rows, (h + 1) * rows)
        base[at, :] = w[at, :] - rate * jnp.dot(own_xt[h], errors, preferred_element_type=jnp.float32)


def pass_kernel(via, far, out, *, half):
    rows = via.shape[0]
    out[...] = (via[...] + far[half * rows : (half + 1) * rows, :].astype(jnp.float32)).astype(out.dtype)


def fold_kernel(place, base, near_a, near_b, out, *, rate):
    rows = near_a.shape[0]
    for half, near in ((place[1], near_b), (1 - place[1], near_a)):
        at = pl.ds(pl.multiple_of(half * rows, rows), rows)
        out[at, :] = base[at, :] - rate * near[...].astype(jnp.float32)


def finish_kernel(place, base, sum_a, sum_b, out, *, rate):
    rows = sum_a.shape[0]
    for half, total in ((place[1], sum_a), (1 - place[1], sum_b)):
        at = pl.ds(pl.multiple_of(half * rows, rows), rows)
        out[at, :] = base[at, :] - rate * total[...].astype(jnp.float32)


def sort_kernel(place, given, order, keep, one, two, three, held):
    del order
    spread, rows, wide = held.shape
    owned = given.shape[0] // (spread * X * Y)
    for at in range(0, rows, 2 * owned):
        block = given[at * spread : (at + 2 * owned) * spread].astype(jnp.float32)
        block = block.reshape(2, spread, owned, wide)
        for i in range(spread):
            held[i, at : at + 2 * owned] = block[:, i].reshape(2 * owned, wide).astype(held.dtype)
    for j, out in enumerate((keep, one, two, three)):
        out[...] = held[place[2] ^ j]


def on_device(tokens, w_key, targets, frag_outer, frag_local, frag_moment):
    rows, width = tokens.shape
    own_rows, columns = w_key.shape
    half = columns // 2
    spots = X * Y
    core = lax.axis_index("c")
    zh = lax.axis_index("zh")
    spot = lax.axis_index("x") * Y + lax.axis_index("y")
    place = jnp.stack([zh, core, lax.axis_index("zl")]).astype(jnp.int32)
    smem = pl.BlockSpec(memory_space=pltpu.SMEM)
    vmem = pl.BlockSpec(memory_space=pltpu.VMEM)
    anywhere = pl.BlockSpec(memory_space=pl.ANY)

    piece = own_rows // spots
    mine = lax.dynamic_slice_in_dim(w_key, spot * piece, piece, 0).astype(jnp.bfloat16)
    column = lax.all_gather(mine, ("zh", "c"), axis=0, tiled=True)
    part = lax.dynamic_slice_in_dim(column, core * half, half, 1).reshape(ZH * 2, piece, half)
    copies = jnp.broadcast_to(part[None], (spots,) + part.shape)
    key = lax.all_to_all(copies, ("x", "y"), 0, 0, tiled=True)

    mate = lax.ppermute(tokens, "c", SWAP)
    goal = lax.ppermute(targets, "c", SWAP)

    def turned(pieces):
        return jax.ShapeDtypeStruct((pieces, own_rows // 2, 2 * rows), jnp.bfloat16)

    far_xt, near_xt, own_xt, both = pl.pallas_call(
        transpose_kernel,
        out_shape=(turned(2), turned(4), turned(2), jax.ShapeDtypeStruct((2 * rows, width + half), jnp.bfloat16)),
        in_specs=[smem] + [vmem] * 4 + [anywhere],
        out_specs=(vmem,) * 4,
        compiler_params=PARAMS,
        cost_estimate=cost(0, 16 * rows * width),
    )(place, tokens, targets, mate, goal, column)

    owned, wide = frag_outer.shape
    block = jax.ShapeDtypeStruct((spots * owned, wide), jnp.bfloat16)
    parts = pl.pallas_call(
        sort_kernel,
        out_shape=(block,) * ZL,
        in_specs=[smem, vmem, anywhere],
        out_specs=(vmem,) * ZL,
        scratch_shapes=[pltpu.VMEM((ZL,) + block.shape, block.dtype)],
        compiler_params=PARAMS,
    )(place, frag_local, column)
    parts = [lax.ppermute(p, "zl", [(i, i ^ j) for i in range(ZL)]) if j else p for j, p in enumerate(parts)]
    err = pl.pallas_call(
        error_kernel,
        out_shape=jax.ShapeDtypeStruct((2 * rows, half), jnp.bfloat16),
        in_specs=[vmem] * 2,
        out_specs=vmem,
        compiler_params=PARAMS,
        cost_estimate=cost(4 * rows * width * half, 8 * rows * width),
    )(both, key)
    err_mate = lax.ppermute(err, "c", SWAP)
    rate = INNER_RATE / width
    short = jax.ShapeDtypeStruct((own_rows // 2, columns), jnp.bfloat16)
    middle = jax.ShapeDtypeStruct((own_rows // 2, columns), jnp.float32)
    long = jax.ShapeDtypeStruct((own_rows, columns), jnp.bfloat16)
    full = jax.ShapeDtypeStruct((own_rows, columns), jnp.float32)
    out = pl.pallas_call(
        far_kernel,
        out_shape=long,
        in_specs=[smem] + [vmem] * 3 + [anywhere] * 3,
        out_specs=vmem,
        compiler_params=PARAMS,
    )(place, far_xt, err, err_mate, *parts[1:])

    far = round_z(out, 0)
    via_a, near_a, via_b, near_b, base, part = pl.pallas_call(
        functools.partial(near_kernel, rate=rate),
        out_shape=(middle, short, middle, short, full, jax.ShapeDtypeStruct(block.shape, jnp.float32)),
        in_specs=[smem] + [vmem] * (5 + ZL) + [anywhere],
        out_specs=(vmem,) * 6,
        compiler_params=PARAMS,
    )(place, near_xt, own_xt, err, err_mate, w_key, *parts, out)
    near_a = round_z(near_a, 0)
    near_b = round_z(near_b, 1)

    def passed(via, half):
        return pl.pallas_call(
            functools.partial(pass_kernel, half=half),
            out_shape=short,
            in_specs=[vmem] * 2,
            out_specs=vmem,
            compiler_params=PARAMS,
        )(via, far)

    sum_a = round_z(passed(via_a, 0), 0)
    sum_b = round_z(passed(via_b, 1), 1)
    base = pl.pallas_call(
        functools.partial(fold_kernel, rate=rate),
        out_shape=full,
        in_specs=[smem] + [vmem] * 3,
        out_specs=vmem,
        compiler_params=PARAMS,
    )(place, base, near_a, near_b)
    new_key = pl.pallas_call(
        functools.partial(finish_kernel, rate=rate),
        out_shape=full,
        in_specs=[smem] + [vmem] * 3,
        out_specs=vmem,
        compiler_params=PARAMS,
    )(place, base, sum_a, sum_b)

    part = lax.all_to_all(part.reshape(spots, owned, wide), ("x", "y"), 0, 0, tiled=True)
    mean = frag_outer - part.sum(0) / (spots * ZL)
    new_moment = MOMENTUM * frag_moment + mean
    new_outer = frag_outer - OUTER_RATE * (mean + MOMENTUM * new_moment)
    return (new_key, new_outer, new_moment)


def solution(mesh):
    grid = Mesh(mesh.devices.reshape(X, Y, ZL, ZH, 2), ("x", "y", "zl", "zh", "c"))
    replica, fsdp = ("x", "y", "zl"), ("zh", "c")
    in_specs = (
        P(replica + fsdp, None),
        P(fsdp, None),
        P(replica + fsdp, None),
        P(fsdp + replica, None),
        P(replica + fsdp, None),
        P(fsdp + replica, None),
    )
    out_specs = (
        P(replica + fsdp, None),
        P(fsdp + replica, None),
        P(fsdp + replica, None),
    )
    return jax.shard_map(
        on_device, mesh=grid, in_specs=in_specs, out_specs=out_specs, check_vma=False
    )
```

```python
import functools

import jax
import jax.numpy as jnp
from jax import lax
from jax.experimental import pallas as pl
from jax.experimental.pallas import tpu as pltpu
from jax.sharding import Mesh, PartitionSpec as P

INNER_RATE = 4.0
OUTER_RATE = 0.7
MOMENTUM = 0.9

X, Y, ZL, ZH = 4, 4, 4, 4
PARAMS = pltpu.CompilerParams(vmem_limit_bytes=16 * 1024 * 1024)
SWAP = [(0, 1), (1, 0)]


def cost(flops, touched):
    return pl.CostEstimate(flops=flops, bytes_accessed=touched, transcendentals=0)


def round_z(a, cross):
    pairs = []
    for zl in range(ZL):
        for zh in range(ZH):
            for core in range(2):
                there = (zh + 1 - 2 * (core ^ (zl & 1))) % ZH
                pairs.append(((zl * ZH + zh) * 2 + core, (zl * ZH + there) * 2 + (core ^ cross)))
    return lax.ppermute(a, ("zl", "zh", "c"), pairs)


def transpose_kernel(place, own, targets, mate, goal, order, far_xt, near_xt, own_xt, both):
    del order
    zh, core = place[0], place[1]
    other = 1 - core
    width = far_xt.shape[1]
    tokens, deep = own.shape
    half = targets.shape[1] // 2
    both[:tokens, :deep] = own[...]
    both[tokens:, :deep] = mate[...]
    columns = pl.ds(pl.multiple_of(core * half, half), half)
    both[:tokens, deep:] = targets[:, columns]
    both[tokens:, deep:] = goal[:, columns]
    far = lax.rem(zh + 2, ZH)
    near = lax.rem(zh + 1 + 2 * (core ^ (place[2] & 1)), ZH)
    for out, places in (
        (far_xt, ((far, core, core), (far, other, core))),
        (near_xt, ((near, core, core), (near, core, other), (near, other, core), (near, other, other))),
        (own_xt, ((zh, core, 0), (zh, core, 1))),
    ):
        for j, (chip, block, half) in enumerate(places):
            columns = pl.ds(pl.multiple_of(((chip * 2 + block) * 2 + half) * width, width), width)
            out[j, :, :tokens] = own[:, columns].T
            out[j, :, tokens:] = mate[:, columns].T


def error_kernel(both, w, out):
    shards, depth = w.shape[1], w.shape[0] * w.shape[2]
    tokens = both.shape[0] // 2
    width = w.shape[3]
    for i in range(2):
        at = slice(i * tokens, (i + 1) * tokens)
        keys = jnp.zeros((tokens, width), jnp.float32)
        for f in range(shards):
            keys += jnp.dot(
                both[at, f * depth : (f + 1) * depth],
                w[:, f].reshape(depth, width),
                preferred_element_type=jnp.float32,
            )
        errors = keys - both[at, shards * depth :].astype(jnp.float32)
        out[at, :] = errors.astype(jnp.bfloat16)


def swapped(err_mate):
    tokens = err_mate.shape[0] // 2
    return jnp.concatenate([err_mate[tokens:, :], err_mate[:tokens, :]], axis=0)


def in_order(place, mine, other):
    low = jnp.where(place[1] == 0, mine, other)
    high = jnp.where(place[1] == 0, other, mine)
    return jnp.concatenate([low, high], axis=1)


def product(xt, errors):
    return jnp.dot(xt, errors, preferred_element_type=jnp.float32)


def far_kernel(xt, err_own, out):
    rows = xt.shape[1]
    for i in range(2):
        out[i * rows : (i + 1) * rows, :] = product(xt[i], err_own[...]).astype(out.dtype)


def second_kernel(place, far_xt, near_xt, err_own, err_mate, one, two, three, out):
    del one, two, three
    other = swapped(err_mate)
    rows, half = far_xt.shape[1], err_own.shape[1]
    near = product(near_xt[1], in_order(place, err_own[...], other)).astype(out.dtype)
    for i in range(2):
        at = slice(i * rows, (i + 1) * rows)
        out[at, :half] = product(far_xt[i], other).astype(out.dtype)
        out[at, half:] = near[:, i * half : (i + 1) * half]


def near_kernel(place, xt, own_xt, err_own, err_mate, w, *refs, rate):
    parts, (_, via_a, via_b, near_b, base, total) = refs[:ZL], refs[ZL:]
    keep, one, two, three = (p[...].astype(jnp.float32) for p in parts)
    total[...] = (keep + one) + (two + three)
    errors = in_order(place, err_own[...], swapped(err_mate))
    for i, out in ((0, via_a), (2, via_b), (3, near_b)):
        out[...] = product(xt[i], errors).astype(out.dtype)
    rows = xt.shape[1]
    for h in range(2):
        at = slice(h * rows, (h + 1) * rows)
        base[at, :] = w[at, :] - rate * product(own_xt[h], errors)


def pass_kernel(place, via, far, second, out, *, half):
    rows = via.shape[0]
    at = slice(half * rows, (half + 1) * rows)
    width = far.shape[1]
    grad = in_order(place, far[at, :].astype(jnp.float32), second[at, :width].astype(jnp.float32))
    out[...] = (via[...] + grad).astype(out.dtype)


def fold_kernel(place, base, second, near_b, out, *, rate):
    rows, width = near_b.shape
    near_a = jnp.concatenate([second[:rows, width // 2 :], second[rows:, width // 2 :]], axis=1)
    for half, near in ((place[1], near_b[...]), (1 - place[1], near_a)):
        at = pl.ds(pl.multiple_of(half * rows, rows), rows)
        out[at, :] = base[at, :] - rate * near.astype(jnp.float32)


def finish_kernel(place, base, sum_a, sum_b, out, *, rate):
    rows = sum_a.shape[0]
    for half, total in ((place[1], sum_a), (1 - place[1], sum_b)):
        at = pl.ds(pl.multiple_of(half * rows, rows), rows)
        out[at, :] = base[at, :] - rate * total[...].astype(jnp.float32)


def copy_kernel(given, order, out):
    del order
    out[...] = given[...]


def sort_kernel(place, given, order, keep, one, two, three, held):
    del order
    spread, rows, wide = held.shape
    owned = given.shape[0] // (spread * X * Y)
    for at in range(0, rows, 2 * owned):
        block = given[at * spread : (at + 2 * owned) * spread].astype(jnp.float32)
        block = block.reshape(2, spread, owned, wide)
        for i in range(spread):
            held[i, at : at + 2 * owned] = block[:, i].reshape(2 * owned, wide).astype(held.dtype)
    for j, out in enumerate((keep, one, two, three)):
        out[...] = held[place[2] ^ j]


def on_device(tokens, w_key, targets, frag_outer, frag_local, frag_moment):
    rows, width = tokens.shape
    own_rows, columns = w_key.shape
    half = columns // 2
    spots = X * Y
    core = lax.axis_index("c")
    zh = lax.axis_index("zh")
    spot = lax.axis_index("x") * Y + lax.axis_index("y")
    place = jnp.stack([zh, core, lax.axis_index("zl")]).astype(jnp.int32)
    smem = pl.BlockSpec(memory_space=pltpu.SMEM)
    vmem = pl.BlockSpec(memory_space=pltpu.VMEM)
    anywhere = pl.BlockSpec(memory_space=pl.ANY)

    piece = own_rows // spots
    mine = lax.dynamic_slice_in_dim(w_key, spot * piece, piece, 0).astype(jnp.bfloat16)
    column = lax.all_gather(mine, ("zh", "c"), axis=0, tiled=True)
    part = lax.dynamic_slice_in_dim(column, core * half, half, 1).reshape(ZH * 2, piece, half)
    copies = jnp.broadcast_to(part[None], (spots,) + part.shape)
    key = lax.all_to_all(copies, ("x", "y"), 0, 0, tiled=True)

    mate = lax.ppermute(tokens, "c", SWAP)
    goal = lax.ppermute(targets, "c", SWAP)

    def turned(pieces):
        return jax.ShapeDtypeStruct((pieces, own_rows // 2, 2 * rows), jnp.bfloat16)

    far_xt, near_xt, own_xt, both = pl.pallas_call(
        transpose_kernel,
        out_shape=(turned(2), turned(4), turned(2), jax.ShapeDtypeStruct((2 * rows, width + half), jnp.bfloat16)),
        in_specs=[smem] + [vmem] * 4 + [anywhere],
        out_specs=(vmem,) * 4,
        compiler_params=PARAMS,
        cost_estimate=cost(0, 16 * rows * width),
    )(place, tokens, targets, mate, goal, column)

    owned, wide = frag_outer.shape
    block = jax.ShapeDtypeStruct((spots * owned, wide), jnp.bfloat16)
    parts = pl.pallas_call(
        sort_kernel,
        out_shape=(block,) * ZL,
        in_specs=[smem, vmem, anywhere],
        out_specs=(vmem,) * ZL,
        scratch_shapes=[pltpu.VMEM((ZL,) + block.shape, block.dtype)],
        compiler_params=PARAMS,
    )(place, frag_local, column)
    parts = [lax.ppermute(p, "zl", [(i, i ^ j) for i in range(ZL)]) if j else p for j, p in enumerate(parts)]
    err = pl.pallas_call(
        error_kernel,
        out_shape=jax.ShapeDtypeStruct((2 * rows, half), jnp.bfloat16),
        in_specs=[vmem] * 2,
        out_specs=vmem,
        compiler_params=PARAMS,
        cost_estimate=cost(4 * rows * width * half, 8 * rows * width),
    )(both, key)
    rate = INNER_RATE / width
    short = jax.ShapeDtypeStruct((own_rows // 2, columns), jnp.bfloat16)
    middle = jax.ShapeDtypeStruct((own_rows // 2, columns), jnp.float32)
    long = jax.ShapeDtypeStruct((own_rows, columns), jnp.bfloat16)
    full = jax.ShapeDtypeStruct((own_rows, columns), jnp.float32)
    far = pl.pallas_call(
        far_kernel,
        out_shape=jax.ShapeDtypeStruct((own_rows, half), jnp.bfloat16),
        in_specs=[vmem] * 2,
        out_specs=vmem,
        compiler_params=PARAMS,
    )(far_xt, err)
    far = round_z(far, 0)
    err_mate = lax.ppermute(err, "c", SWAP)
    out = pl.pallas_call(
        second_kernel,
        out_shape=long,
        in_specs=[smem] + [vmem] * 4 + [anywhere] * 3,
        out_specs=vmem,
        compiler_params=PARAMS,
        cost_estimate=cost(0, 64 * rows * width),
    )(place, far_xt, near_xt, err, err_mate, *parts[1:])
    second = round_z(out, 0)
    via_a, via_b, near_b, base, part = pl.pallas_call(
        functools.partial(near_kernel, rate=rate),
        out_shape=(middle, middle, short, full, jax.ShapeDtypeStruct(block.shape, jnp.float32)),
        in_specs=[smem] + [vmem] * (5 + ZL) + [anywhere],
        out_specs=(vmem,) * 5,
        compiler_params=PARAMS,
    )(place, near_xt, own_xt, err, err_mate, w_key, *parts, out)
    near_b = round_z(near_b, 1)
    part = pl.pallas_call(
        copy_kernel,
        out_shape=jax.ShapeDtypeStruct(block.shape, jnp.float32),
        in_specs=[vmem, anywhere],
        out_specs=vmem,
        compiler_params=PARAMS,
    )(part, far)

    def passed(via, half):
        return pl.pallas_call(
            functools.partial(pass_kernel, half=half),
            out_shape=short,
            in_specs=[smem] + [vmem] * 3,
            out_specs=vmem,
            compiler_params=PARAMS,
        )(place, via, far, second)

    sum_a = round_z(passed(via_a, 0), 0)
    sum_b = round_z(passed(via_b, 1), 1)
    base = pl.pallas_call(
        functools.partial(fold_kernel, rate=rate),
        out_shape=full,
        in_specs=[smem] + [vmem] * 3,
        out_specs=vmem,
        compiler_params=PARAMS,
    )(place, base, second, near_b)
    new_key = pl.pallas_call(
        functools.partial(finish_kernel, rate=rate),
        out_shape=full,
        in_specs=[smem] + [vmem] * 3,
        out_specs=vmem,
        compiler_params=PARAMS,
    )(place, base, sum_a, sum_b)

    part = lax.all_to_all(part.reshape(spots, owned, wide), ("x", "y"), 0, 0, tiled=True)
    mean = frag_outer - part.sum(0) / (spots * ZL)
    new_moment = MOMENTUM * frag_moment + mean
    new_outer = frag_outer - OUTER_RATE * (mean + MOMENTUM * new_moment)
    return (new_key, new_outer, new_moment)


def solution(mesh):
    grid = Mesh(mesh.devices.reshape(X, Y, ZL, ZH, 2), ("x", "y", "zl", "zh", "c"))
    replica, fsdp = ("x", "y", "zl"), ("zh", "c")
    in_specs = (
        P(replica + fsdp, None),
        P(fsdp, None),
        P(replica + fsdp, None),
        P(fsdp + replica, None),
        P(replica + fsdp, None),
        P(fsdp + replica, None),
    )
    out_specs = (
        P(replica + fsdp, None),
        P(fsdp + replica, None),
        P(fsdp + replica, None),
    )
    return jax.shard_map(
        on_device, mesh=grid, in_specs=in_specs, out_specs=out_specs, check_vma=False
    )
```
